128 devices in a mesh: row: 16 (over z_hi, y, core), col: 8 (over x, z_lo).
Axes of the slice: x: 4, y: 4, z: 4 (z_hi: 2, z_lo: 2; z = z_hi * 2 + z_lo), core: 2. Of those that a mesh axis runs over, the one named last changes fastest.
Arguments:
- inputs: bfloat16 [4, 65536, 1024], P(None, ('row', 'col')), may hold values from -36 to 36
- cotangents: bfloat16 [4, 65536, 1024], P(None, ('row', 'col')), may hold values from -0.5745243 to 0.5745243
- error_buffer: bfloat16 [128, 4, 1024, 1024], P(('row', 'col')), may hold values from -24 to 24
- previous_q: float32 [4, 32, 1024], replicated, may hold values from -6 to 6
Outputs:
- new_error: bfloat16 [128, 4, 1024, 1024], P(('row', 'col'))
- update: bfloat16 [4, 1024, 1024], P(None, ('row', 'col'))
- new_q: float32 [4, 32, 1024], replicated
The draws below stay inside these ranges and needn't reach their ends.
All inputs are finite; a program needn't handle non-finite values.
Results may differ from the reference program's by a relative error of at most 0.001.
Values sent between devices are 32-bit elements; how exact they have to be, the bound alone decides.
No kernel may reach another device: no remote copies, remote signals or barrier semaphores. Data moves between devices by JAX's collectives and lax.ppermute only.
A program may use at most 128 MiB of HBM per device.

```python
import math
import jax
import jax.numpy as jnp
from jax import lax

D = 1024
R = 32
MATS = 4
TOK_DEV = 512
REPLICAS = 128
TOKENS = 65536


def spread_scales(key, shape, lower, upper):
    return jnp.exp(jax.random.uniform(key, shape, jnp.float32, math.log(lower), math.log(upper)))


def draw_inputs(key, part):
    key = jax.random.fold_in(key, 11)
    key_scale, key_common, key_noise = jax.random.split(key, 3)
    position = jnp.arange(D, dtype=jnp.float32) / D
    scale = 10.0 ** (position - 0.5) * spread_scales(key_scale, (MATS, 1, D), 0.7, 1.4)
    common = jnp.clip(jax.random.normal(key_common, (MATS, TOK_DEV, D), jnp.float32), -4.0, 4.0)
    noise = jnp.clip(jax.random.normal(key_noise, (MATS, TOKENS, D), jnp.float32), -4.0, 4.0)
    values = (jnp.tile(common, (1, TOKENS // TOK_DEV, 1)) + noise) * scale
    return values.astype(jnp.bfloat16)


def draw_cotangents(key, part):
    key = jax.random.fold_in(key, 12)
    key_scale, key_common, key_noise = jax.random.split(key, 3)
    scale = spread_scales(key_scale, (MATS, 1, D), 0.32, 3.2) * (0.5 / TOK_DEV ** 0.5)
    common = jnp.clip(jax.random.normal(key_common, (MATS, TOK_DEV, D), jnp.float32), -4.0, 4.0)
    noise = jnp.clip(jax.random.normal(key_noise, (MATS, TOKENS, D), jnp.float32), -4.0, 4.0)
    values = (jnp.tile(common, (1, TOKENS // TOK_DEV, 1)) + noise) * scale
    return values.astype(jnp.bfloat16)


def raised(array, own_key, source, target, parts, factor):
    def block_of(dim):
        return (jnp.arange(array.shape[dim]) // (array.shape[dim] // parts)).reshape((-1,) + (1,) * (array.ndim - 1 - dim))

    first = jax.random.permutation(own_key, parts)[block_of(target)]
    far = (block_of(target) + parts // 2) % parts
    return jnp.where((block_of(source) == first) | (block_of(source) == far), factor * array, array)


def levels(rng, extent, cuts, low, top_value):
    def one(axis_at, blocks):
        heights = jax.random.uniform(jax.random.fold_in(jax.random.fold_in(rng, 6), axis_at), (blocks,), jnp.float32, low / len(cuts), top_value / len(cuts))
        return jnp.repeat(jnp.exp(heights), extent[axis_at] // blocks).reshape((-1,) + (1,) * (len(extent) - axis_at - 1))

    loudness = one(*cuts[0])
    for cut in cuts[1:]:
        loudness = loudness * one(*cut)
    return loudness


def gaussian(key, shape, width, reach, cuts=(), held_as=jnp.bfloat16):
    drawn = jax.random.normal(key, shape, jnp.float32) * width
    if len(cuts) > 0:
        drawn = levels(key, shape, cuts, -0.22, 0.18) * drawn
    return jnp.clip(drawn, min=-reach, max=reach).astype(held_as)


def bell_draw_with(key, extent, deviation, limit, shards, heavy, kind=jnp.bfloat16):
    result = deviation * jax.random.normal(key, extent, jnp.float32)
    if shards:
        result = result * levels(key, extent, shards, -0.22, 0.18)
    return jnp.clip(raised(result, jax.random.fold_in(key, 3), *heavy), -limit, limit).astype(kind)


def setup_inputs(seed: int = 0) -> dict:
    key_of = jax.random.split(jax.random.key(seed), 5)
    return {
        "inputs": draw_inputs(jax.random.fold_in(key_of[4], 71), 0),
        "cotangents": draw_cotangents(jax.random.fold_in(key_of[4], 71), 0),
        "error_buffer": bell_draw_with(key_of[2], (REPLICAS, MATS, D, D), 1.0, 24.0, ((0, 128),), (0, 2, 128, 5.5)),
        "previous_q": gaussian(key_of[3], (MATS, R, D), 1.0, 6.0, (), jnp.float32),
    }


def gram_schmidt(p_rows):
    finished = []
    for column in range(p_rows.shape[1]):
        vector = p_rows[:, column, :]
        for earlier in finished:
            vector = vector - lax.optimization_barrier(jnp.sum(earlier * vector, axis=-1, keepdims=True)) * earlier
        vector = vector / jnp.sqrt(lax.optimization_barrier(jnp.sum(vector * vector, axis=-1, keepdims=True)) + 1e-06)
        finished.append(vector)
    return jnp.stack(finished, axis=1)

def reference(inputs, cotangents, error_buffer, previous_q):
    highest = lax.Precision.HIGHEST
    acts = inputs.reshape(MATS, REPLICAS, TOK_DEV, D).transpose(1, 0, 2, 3)
    cots = cotangents.reshape(MATS, REPLICAS, TOK_DEV, D).transpose(1, 0, 2, 3)

    def merge_one(pieces):
        activation, cotangent, carried = pieces
        grads = jnp.einsum('mti,mtj->mij', activation.astype(jnp.float32), cotangent.astype(jnp.float32), precision=highest)
        return grads + carried.astype(jnp.float32)
    merged = lax.map(merge_one, (acts, cots, error_buffer))
    p_mean = jnp.einsum('mrj,nmij->mri', previous_q, merged, precision=highest) / REPLICAS
    basis = gram_schmidt(p_mean)
    new_q = jnp.einsum('mri,nmij->mrj', basis, merged, precision=highest) / REPLICAS
    decompressed = jnp.einsum('mri,mrj->mij', basis, new_q, precision=highest)
    new_error = (merged - decompressed[None]).astype(jnp.bfloat16)
    return (new_error, decompressed.astype(jnp.bfloat16), new_q)
```

```python
import jax
import jax.numpy as jnp
from jax import lax
from jax.experimental import pallas as pl
from jax.experimental.pallas import tpu as pltpu
from jax.sharding import PartitionSpec as P

AXES = ("row", "col")
SIZES = (("zh", 2), ("y", 4), ("core", 2), ("x", 4), ("zl", 2))
MATCHINGS = (("x", 0), ("y", 0), ("z", 0), ("x", 1), ("y", 1), ("z", 1))
FIRST = ((0, 3), (1, 4))


def coords_of(index):
    coords = {}
    for name, size in reversed(SIZES):
        coords[name] = index % size
        index //= size
    return coords


def index_of(coords):
    index = 0
    for name, size in SIZES:
        index = index * size + coords[name]
    return index


def partner(index, matching):
    coords = coords_of(index)
    axis, odd = matching
    if axis == "z":
        z = 2 * coords["zh"] + coords["zl"]
        z = 3 - z if odd else z ^ 1
        coords["zh"], coords["zl"] = z // 2, z % 2
    else:
        coords[axis] = 3 - coords[axis] if odd else coords[axis] ^ 1
    return index_of(coords)


def step_pairs(flow, step):
    pairs = []
    for index in range(128):
        first = FIRST[flow][coords_of(index)["core"]]
        pairs.append((index, partner(index, MATCHINGS[(first + step) % 6])))
    return pairs


def core_pairs():
    pairs = []
    for index in range(128):
        coords = coords_of(index)
        coords["core"] ^= 1
        pairs.append((index, index_of(coords)))
    return pairs


def other_core(value):
    return lax.ppermute(value, AXES, core_pairs())


MIB = 1024 * 1024
VMEM = pl.BlockSpec(memory_space=pltpu.VMEM)
HBM = pl.BlockSpec(memory_space=pltpu.HBM)
ANY = pl.BlockSpec(memory_space=pl.ANY)
SMEM = pl.BlockSpec(memory_space=pltpu.SMEM)
CHUNK = 256
F32 = jnp.float32
BF16 = jnp.bfloat16


def shape(*dims, dtype=F32):
    return jax.ShapeDtypeStruct(dims, dtype)


def params(mib):
    return pltpu.CompilerParams(vmem_limit_bytes=mib * MIB)


def cost(flops, mib):
    return pl.CostEstimate(flops=flops, bytes_accessed=int(mib * MIB), transcendentals=0)


def terms(value, count):
    parts = []
    for _ in range(count):
        part = value.astype(BF16)
        parts.append(part)
        value = value - part.astype(F32)
    return parts


def split(value, count):
    return jnp.concatenate(terms(value, count), 0)


def folded(value, count):
    rows = value.shape[0] // count
    total = value[:rows]
    for n in range(1, count):
        total = total + value[n * rows : (n + 1) * rows]
    return total


def dot(a, b, contract):
    return lax.dot_general(a, b, ((contract[:1], contract[1:]), ((), ())), preferred_element_type=F32)


def members(scalars_ref, flow):
    core = scalars_ref[0]
    return 2 * (1 - core) + flow, 2 * core + flow


def load_kernel(flow, scalars_ref, x_hbm, c_hbm, e_hbm, q_hbm, after_ref, x_ref, c_ref, e_ref, other_ref, own_ref, q_ref, sems):
    copies = []
    for slot, m in enumerate(members(scalars_ref, flow)):
        parts = [
            (q_hbm.at[m], q_ref.at[slot]),
            (c_hbm.at[m], c_ref.at[slot]),
            (x_hbm.at[m], x_ref.at[slot]),
        ] + [(e_hbm.at[0, m, pl.ds(n, 256)], e_ref.at[slot, pl.ds(n, 256)]) for n in range(0, 1024, 256)]
        started = []
        for n, (source, target) in enumerate(parts):
            copy = pltpu.make_async_copy(source, target, sems.at[slot, n])
            copy.start()
            started.append(copy)
        copies.append(started)
    for slot, out_ref in enumerate((other_ref, own_ref)):
        copies[slot][0].wait()
        q = split(q_ref[slot], 3)
        copies[slot][1].wait()
        y = split(folded(dot(q, c_ref[slot], (1, 1)), 3), 3)
        copies[slot][2].wait()
        out_ref[...] = folded(dot(y, x_ref[slot], (1, 0)), 3)
        for n in range(4):
            copies[slot][3 + n].wait()
            rows = pl.ds(256 * n, 256)
            out_ref[:, rows] += folded(dot(q, e_ref[slot, rows], (1, 1)), 3)


def load(flow, scalars, arrays, after):
    return pl.pallas_call(
        lambda *refs: load_kernel(flow, *refs),
        out_shape=[
            pltpu.VMEM((2, 512, 1024), BF16),
            pltpu.VMEM((2, 512, 1024), BF16),
            pltpu.VMEM((2, 1024, 1024), BF16),
            shape(32, 1024),
            shape(32, 1024),
        ],
        in_specs=[SMEM, HBM, HBM, HBM, HBM, ANY],
        out_specs=[VMEM] * 5,
        scratch_shapes=[pltpu.VMEM((2, 32, 1024), F32), pltpu.SemaphoreType.DMA((2, 7))],
        compiler_params=params(6),
        cost_estimate=cost(2 * 2 * 96 * 1024 * 2048, 9),
    )(scalars, *arrays, after)


def project_kernel(slot, x_ref, c_ref, e_ref, p_ref, after_ref, z_ref):
    p = split(p_ref[...], 3)
    w = split(folded(dot(p, x_ref[slot], (1, 1)), 3), 3)
    z_ref[...] = folded(dot(w, c_ref[slot], (1, 0)) + dot(p, e_ref[slot], (1, 0)), 3)


def project(slot, held, p, after):
    return pl.pallas_call(
        lambda *refs: project_kernel(slot, *refs),
        out_shape=shape(32, 1024),
        in_specs=[VMEM] * 4 + [ANY],
        out_specs=VMEM,
        compiler_params=params(6),
        cost_estimate=cost(2 * 96 * 1024 * 2048, 4),
    )(*held, p, after)


def gram_schmidt_kernel(p_ref, after_ref, basis_ref, factor_ref):
    value = p_ref[...]
    rows = lax.broadcasted_iota(jnp.int32, (32, 128), 0)
    lanes = lax.broadcasted_iota(jnp.int32, (32, 128), 1)
    factor = jnp.where(rows == lanes, 1.0, 0.0)
    for k in range(32):
        group = k // 8 * 8
        if k % 8 == 0 and k > 0:
            value, factor = value[8:], factor[8:]
        at = k - group
        row, factor_row = value[at : at + 1], factor[at : at + 1]
        dots = jnp.sum(value * row, axis=1, keepdims=True)
        square = dots[at : at + 1] + 1e-6
        scale = 1.0 / jnp.sqrt(square)
        basis_ref[k : k + 1, :] = row * scale
        factor_ref[k : k + 1, :] = factor_row * scale
        weights = dots * (1.0 / square)
        value = value - weights * row
        factor = factor - weights * factor_row


def gram_schmidt(p, after):
    return pl.pallas_call(
        gram_schmidt_kernel,
        out_shape=[shape(32, 1024), shape(32, 128)],
        in_specs=[VMEM, ANY],
        out_specs=[VMEM, VMEM],
        compiler_params=params(4),
        cost_estimate=cost(4_000_000, 8),
    )(p, after)


def flip_kernel(scalars_ref, other_ref, own_ref, other_left, own_left, other_rows, own_rows, flipped):
    start = pl.multiple_of(scalars_ref[1] * 8, 8)
    for basis_ref, left_ref, rows_ref in ((other_ref, other_left, other_rows), (own_ref, own_left, own_rows)):
        flipped[...] = basis_ref[...].T
        high, low = terms(flipped[...], 2)
        left_ref[...] = jnp.concatenate([high, high, low], 1)
        high, low = terms(flipped[pl.ds(start, 8), :], 2)
        rows_ref[...] = jnp.concatenate([high, high, low], 1).astype(F32)


def flip(scalars, other_basis, own_basis):
    return pl.pallas_call(
        flip_kernel,
        out_shape=[shape(1024, 96, dtype=BF16)] * 2 + [shape(8, 96)] * 2,
        in_specs=[SMEM, VMEM, VMEM],
        out_specs=[VMEM] * 4,
        scratch_shapes=[pltpu.VMEM((1024, 32), F32)],
        compiler_params=params(4),
        cost_estimate=cost(1_000_000, 3),
    )(scalars, other_basis, own_basis)


def merge_kernel(slot, x_ref, c_ref, e_ref, after_ref, merged_ref):
    for start in range(0, 1024, CHUNK):
        rows = pl.ds(start, CHUNK)
        product = dot(x_ref[slot, :, rows], c_ref[slot], (0, 0))
        merged_ref[rows] = product + e_ref[slot, rows].astype(F32)


def merge(slot, held, after):
    return pl.pallas_call(
        lambda *refs: merge_kernel(slot, *refs),
        out_shape=pltpu.VMEM((1024, 1024), F32),
        in_specs=[VMEM] * 3 + [ANY],
        out_specs=VMEM,
        compiler_params=params(6),
        cost_estimate=cost(2 * 512 * 1024 * 1024, 4),
    )(*held, after)


def solve_kernel(a_ref, b_ref, factor_ref, q_ref):
    f = terms(factor_ref[:, :32], 3)
    z = terms(a_ref[...] + b_ref[...], 3)
    pairs = ((0, 0), (0, 1), (0, 2), (1, 0), (1, 1), (2, 0))
    left = jnp.concatenate([f[i] for i, _ in pairs], 1)
    right = jnp.concatenate([z[j] for _, j in pairs], 0)
    q_ref[...] = dot(left, right, (1, 0)) * (1.0 / 128.0)


def solve(a, b, factor):
    return pl.pallas_call(
        solve_kernel,
        out_shape=shape(32, 1024),
        in_specs=[VMEM] * 3,
        out_specs=VMEM,
        compiler_params=params(4),
        cost_estimate=cost(2 * 32 * 192 * 1024, 1),
    )(a, b, factor)


def finish_flow(flow, scalars_ref, merged, lefts, qs, rows, outs, error_hbm, stage, sems):
    copies = []
    for slot, m in enumerate(members(scalars_ref, flow)):
        high, low = terms(qs[slot][...], 2)
        right = jnp.concatenate([high, low, high], 0)
        for n, start in enumerate(range(0, 1024, CHUNK)):
            block = pl.ds(start, CHUNK)
            product = dot(lefts[slot][block], right, (1, 0))
            stage[slot, block] = (merged[slot][block] - product).astype(BF16)
            copy = pltpu.make_async_copy(stage.at[slot, block], error_hbm.at[0, m, block], sems.at[slot, n])
            copy.start()
            copies.append(copy)
        outs[slot][...] = dot(rows[slot][...].astype(BF16), right, (1, 0))
    return copies


def finish_first_kernel(scalars_ref, *refs):
    merged, lefts, qs, rows = (refs[2 * n : 2 * n + 2] for n in range(4))
    error_hbm, other_out, own_out, stage, sems = refs[8:]
    for copy in finish_flow(0, scalars_ref, merged, lefts, qs, rows, (other_out, own_out), error_hbm, stage, sems):
        copy.wait()


def finish_first(scalars, merged, lefts, qs, rows):
    return pl.pallas_call(
        finish_first_kernel,
        out_shape=[shape(1, 4, 1024, 1024, dtype=BF16)] + [shape(8, 1024)] * 2,
        in_specs=[SMEM] + [VMEM] * 8,
        out_specs=[HBM, VMEM, VMEM],
        scratch_shapes=[pltpu.VMEM((2, 1024, 1024), BF16), pltpu.SemaphoreType.DMA((2, 1024 // CHUNK))],
        compiler_params=params(10),
        cost_estimate=cost(2 * 2 * 256 * 1024 * 1024, 4),
    )(scalars, *merged, *lefts, *qs, *rows)


def finish_last_kernel(scalars_ref, earlier_ref, *refs):
    merged, lefts, qs, rows, first_qs, first_outs = (refs[2 * n : 2 * n + 2] for n in range(6))
    error_hbm, update_hbm, new_q_hbm, outs, update, stage, sems, q_sems, update_sem = refs[12:]
    copies = []
    places = (*members(scalars_ref, 0), *members(scalars_ref, 1))
    for n, (m, q_ref) in enumerate(zip(places, (*first_qs, *qs))):
        copies.append(pltpu.make_async_copy(q_ref, new_q_hbm.at[m], q_sems.at[n]))
    for copy in copies:
        copy.start()
    flow_outs = (outs.at[0], outs.at[1])
    copies += finish_flow(1, scalars_ref, merged, lefts, qs, rows, flow_outs, error_hbm, stage, sems)
    for m, out_ref in zip(places, (*first_outs, *flow_outs)):
        update[m] = out_ref[...].astype(BF16)
    copies.append(pltpu.make_async_copy(update, update_hbm, update_sem))
    copies[-1].start()
    for copy in copies:
        copy.wait()


def finish_last(scalars, error, merged, lefts, qs, rows, first_qs, first_outs):
    return pl.pallas_call(
        finish_last_kernel,
        out_shape=[shape(1, 4, 1024, 1024, dtype=BF16), shape(4, 8, 1024, dtype=BF16), shape(4, 32, 1024)],
        in_specs=[SMEM, HBM] + [VMEM] * 12,
        out_specs=[HBM, HBM, HBM],
        scratch_shapes=[
            pltpu.VMEM((2, 8, 1024), F32),
            pltpu.VMEM((4, 8, 1024), BF16),
            pltpu.VMEM((2, 1024, 1024), BF16),
            pltpu.SemaphoreType.DMA((2, 1024 // CHUNK)),
            pltpu.SemaphoreType.DMA((4,)),
            pltpu.SemaphoreType.DMA,
        ],
        input_output_aliases={1: 0},
        compiler_params=params(10),
        cost_estimate=cost(2 * 2 * 256 * 1024 * 1024, 4),
    )(scalars, error, *merged, *lefts, *qs, *rows, *first_qs, *first_outs)


def other_core(value):
    return lax.ppermute(value, AXES, core_pairs())


def exchange(step, values):
    return [lax.ppermute(values[f], AXES, step_pairs(f, step)) for f in range(2)]


def added(values, received):
    return [a + b for a, b in zip(values, received)]


def on_device(inputs, cotangents, error_buffer, previous_q):
    scalars = jnp.stack([lax.axis_index("row") % 2, lax.axis_index(AXES)]).astype(jnp.int32)
    arrays = [pltpu.with_memory_space_constraint(a, pltpu.HBM) for a in (inputs, cotangents, error_buffer, previous_q)]
    held, sums, merged = [], [], [[None, None], [None, None]]
    after = jnp.zeros((8, 128), F32)
    for flow in range(2):
        *arrays_here, other, own = load(flow, scalars, arrays, after)
        held.append(arrays_here)
        after = own + other_core(other)
        sums.append(after)
    for step in range(6):
        received = exchange(step, sums)
        if step in (1, 2):
            merged[0][step - 1] = merge(step - 1, held[0], sums[1])
        sums = added(sums, received)
    means = [value * (1.0 / 128.0) for value in sums]
    other_means = [other_core(value) for value in means]
    sums, after = [], means[0]
    for flow in range(2):
        own = project(1, held[flow], means[flow], after)
        after = project(0, held[flow], other_means[flow], own)
        sums.append(own + other_core(after))
    bases, factors, lefts, rows = [], [], [], []
    for step in range(6):
        received = exchange(step, sums)
        if step < 2:
            basis, factor = gram_schmidt(means[step], sums[1])
            bases.append(basis)
            factors.append(factor)
        elif step < 4:
            merged[1][step - 2] = merge(step - 2, held[1], sums[1])
        if 1 <= step < 3:
            other_left, own_left, other_rows, own_rows = flip(scalars, other_core(bases[step - 1]), bases[step - 1])
            lefts.append((other_left, own_left))
            rows.append((other_rows, own_rows))
        if step < 5:
            sums = added(sums, received)
    own_qs = [solve(sums[f], received[f], factors[f]) for f in range(2)]
    qs = [(other_core(q), q) for q in own_qs]
    error, *outs = finish_first(scalars, merged[0], lefts[0], qs[0], rows[0])
    return finish_last(scalars, error, merged[1], lefts[1], qs[1], rows[1], qs[0], outs)


def solution(mesh):
    return jax.shard_map(
        on_device,
        mesh=mesh,
        in_specs=(
            P(None, AXES, None),
            P(None, AXES, None),
            P(AXES, None, None, None),
            P(),
        ),
        out_specs=(P(AXES, None, None, None), P(None, AXES, None), P()),
        check_vma=False,
    )
```

```python
import jax
import jax.numpy as jnp
from jax import lax
from jax.experimental import pallas as pl
from jax.experimental.pallas import tpu as pltpu
from jax.sharding import PartitionSpec as P

AXES = ("row", "col")
SIZES = (("zh", 2), ("y", 4), ("core", 2), ("x", 4), ("zl", 2))
ORDERS = (("x", "y", "z"), ("y", "z", "x"))


def coords_of(index):
    coords = {}
    for name, size in reversed(SIZES):
        coords[name] = index % size
        index //= size
    return coords


def index_of(coords):
    index = 0
    for name, size in SIZES:
        index = index * size + coords[name]
    return index


def partner(index, axis, mask):
    coords = coords_of(index)
    if axis == "z":
        z = (2 * coords["zh"] + coords["zl"]) ^ mask
        coords["zh"], coords["zl"] = z // 2, z % 2
    else:
        coords[axis] ^= mask
    return index_of(coords)


def step_pairs(step, mask):
    return [(index, partner(index, ORDERS[coords_of(index)["core"]][step], mask)) for index in range(128)]


def core_pairs():
    pairs = []
    for index in range(128):
        coords = coords_of(index)
        coords["core"] ^= 1
        pairs.append((index, index_of(coords)))
    return pairs


def other_core(value):
    return lax.ppermute(value, AXES, core_pairs())


MIB = 1024 * 1024
VMEM = pl.BlockSpec(memory_space=pltpu.VMEM)
HBM = pl.BlockSpec(memory_space=pltpu.HBM)
ANY = pl.BlockSpec(memory_space=pl.ANY)
SMEM = pl.BlockSpec(memory_space=pltpu.SMEM)
CHUNK = 256
F32 = jnp.float32
BF16 = jnp.bfloat16


def shape(*dims, dtype=F32):
    return jax.ShapeDtypeStruct(dims, dtype)


def params(mib):
    return pltpu.CompilerParams(vmem_limit_bytes=mib * MIB)


def cost(flops, mib):
    return pl.CostEstimate(flops=flops, bytes_accessed=int(mib * MIB), transcendentals=0)


def terms(value, count):
    parts = []
    for _ in range(count):
        part = value.astype(BF16)
        parts.append(part)
        value = value - part.astype(F32)
    return parts


def split(value, count):
    return jnp.concatenate(terms(value, count), 0)


def folded(value, count):
    rows = value.shape[0] // count
    total = value[:rows]
    for n in range(1, count):
        total = total + value[n * rows : (n + 1) * rows]
    return total


def dot(a, b, contract):
    return lax.dot_general(a, b, ((contract[:1], contract[1:]), ((), ())), preferred_element_type=F32)


def members(scalars_ref, side):
    core = scalars_ref[0]
    first = 2 * core if side else 2 * (1 - core)
    return first, first + 1


def load_kernel(side, scalars_ref, x_hbm, c_hbm, e_hbm, q_hbm, x_ref, c_ref, e_ref, p_ref, q_ref, sems):
    copies = []
    for slot, m in enumerate(members(scalars_ref, side)):
        parts = [
            (q_hbm.at[m], q_ref.at[slot]),
            (c_hbm.at[m], c_ref.at[slot]),
            (x_hbm.at[m], x_ref.at[slot]),
        ] + [(e_hbm.at[0, m, pl.ds(n, 512)], e_ref.at[slot, pl.ds(n, 512)]) for n in range(0, 1024, 512)]
        started = []
        for n, (source, target) in enumerate(parts):
            copy = pltpu.make_async_copy(source, target, sems.at[slot, n])
            copy.start()
            started.append(copy)
        copies.append(started)
    for slot in range(2):
        copies[slot][0].wait()
        q = split(q_ref[slot], 3)
        copies[slot][1].wait()
        y = split(folded(dot(q, c_ref[slot], (1, 1)), 3), 3)
        copies[slot][2].wait()
        p_ref[slot] = folded(dot(y, x_ref[slot], (1, 0)), 3)
        for n in range(2):
            copies[slot][3 + n].wait()
            rows = pl.ds(512 * n, 512)
            p_ref[slot, :, rows] += folded(dot(q, e_ref[slot, rows], (1, 1)), 3)


def load(side, scalars, arrays):
    return pl.pallas_call(
        lambda *refs: load_kernel(side, *refs),
        out_shape=[
            pltpu.VMEM((2, 512, 1024), BF16),
            pltpu.VMEM((2, 512, 1024), BF16),
            pltpu.VMEM((2, 1024, 1024), BF16),
            shape(2, 32, 1024),
        ],
        in_specs=[SMEM, HBM, HBM, HBM, HBM],
        out_specs=[VMEM] * 4,
        scratch_shapes=[pltpu.VMEM((2, 32, 1024), F32), pltpu.SemaphoreType.DMA((2, 5))],
        compiler_params=params(6),
        cost_estimate=cost(2 * 2 * 96 * 1024 * 2048, 9),
    )(scalars, *arrays)


def project_kernel(x_ref, c_ref, e_ref, p_ref, after_ref, z_ref):
    for slot in range(2):
        p = split(p_ref[slot], 3)
        w = split(folded(dot(p, x_ref[slot], (1, 1)), 3), 3)
        z_ref[slot] = folded(dot(w, c_ref[slot], (1, 0)) + dot(p, e_ref[slot], (1, 0)), 3)


def project(held, p, after):
    return pl.pallas_call(
        project_kernel,
        out_shape=shape(2, 32, 1024),
        in_specs=[VMEM] * 4 + [ANY],
        out_specs=VMEM,
        compiler_params=params(6),
        cost_estimate=cost(2 * 2 * 96 * 1024 * 2048, 8),
    )(*held, p, after)


def gram_schmidt_kernel(slot, p_ref, after_ref, basis_ref, factor_ref):
    value = p_ref[slot]
    rows = lax.broadcasted_iota(jnp.int32, (32, 128), 0)
    lanes = lax.broadcasted_iota(jnp.int32, (32, 128), 1)
    factor = jnp.where(rows == lanes, 1.0, 0.0)
    for k in range(32):
        group = k // 8 * 8
        if k % 8 == 0 and k > 0:
            value, factor = value[8:], factor[8:]
        at = k - group
        row, factor_row = value[at : at + 1], factor[at : at + 1]
        dots = jnp.sum(value * row, axis=1, keepdims=True)
        square = dots[at : at + 1] + 1e-6
        scale = 1.0 / jnp.sqrt(square)
        basis_ref[k : k + 1, :] = row * scale
        factor_ref[k : k + 1, :] = factor_row * scale
        weights = dots * (1.0 / square)
        value = value - weights * row
        factor = factor - weights * factor_row


def gram_schmidt(slot, p, after):
    return pl.pallas_call(
        lambda *refs: gram_schmidt_kernel(slot, *refs),
        out_shape=[shape(32, 1024), shape(32, 128)],
        in_specs=[VMEM, ANY],
        out_specs=[VMEM, VMEM],
        compiler_params=params(4),
        cost_estimate=cost(4_000_000, 8),
    )(p, after)


def flip_kernel(scalars_ref, first_ref, second_ref, after_ref, first_left, second_left, first_rows, second_rows, flipped):
    start = pl.multiple_of(scalars_ref[1] * 8, 8)
    for basis_ref, left_ref, rows_ref in ((first_ref, first_left, first_rows), (second_ref, second_left, second_rows)):
        flipped[...] = basis_ref[...].T
        high, low = terms(flipped[...], 2)
        left_ref[...] = jnp.concatenate([high, high, low], 1)
        high, low = terms(flipped[pl.ds(start, 8), :], 2)
        rows_ref[...] = jnp.concatenate([high, high, low], 1).astype(F32)


def flip(scalars, bases, after):
    return pl.pallas_call(
        flip_kernel,
        out_shape=[shape(1024, 96, dtype=BF16)] * 2 + [shape(8, 96)] * 2,
        in_specs=[SMEM, VMEM, VMEM, ANY],
        out_specs=[VMEM] * 4,
        scratch_shapes=[pltpu.VMEM((1024, 32), F32)],
        compiler_params=params(4),
        cost_estimate=cost(1_000_000, 3),
    )(scalars, *bases, after)


def merge_kernel(slot, x_ref, c_ref, e_ref, after_ref, merged_ref):
    for start in range(0, 1024, CHUNK):
        rows = pl.ds(start, CHUNK)
        product = dot(x_ref[slot, :, rows], c_ref[slot], (0, 0))
        merged_ref[rows] = product + e_ref[slot, rows].astype(F32)


def merge(slot, held, after):
    return pl.pallas_call(
        lambda *refs: merge_kernel(slot, *refs),
        out_shape=pltpu.VMEM((1024, 1024), F32),
        in_specs=[VMEM] * 3 + [ANY],
        out_specs=VMEM,
        compiler_params=params(6),
        cost_estimate=cost(2 * 512 * 1024 * 1024, 4),
    )(*held, after)


def solve_kernel(total_ref, first_ref, second_ref, q_ref):
    pairs = ((0, 0), (0, 1), (0, 2), (1, 0), (1, 1), (2, 0))
    for slot, factor_ref in enumerate((first_ref, second_ref)):
        f = terms(factor_ref[:, :32], 3)
        z = terms(total_ref[slot], 3)
        left = jnp.concatenate([f[i] for i, _ in pairs], 1)
        right = jnp.concatenate([z[j] for _, j in pairs], 0)
        q_ref[slot] = dot(left, right, (1, 0)) * (1.0 / 128.0)


def solve(total, factors):
    return pl.pallas_call(
        solve_kernel,
        out_shape=shape(2, 32, 1024),
        in_specs=[VMEM] * 3,
        out_specs=VMEM,
        compiler_params=params(4),
        cost_estimate=cost(2 * 2 * 32 * 192 * 1024, 1),
    )(total, *factors)


def finish_kernel(side, scalars_ref, merged, lefts, q_ref, rows, error_hbm, stage, sems):
    copies, outs = [], []
    for slot, m in enumerate(members(scalars_ref, side)):
        high, low = terms(q_ref[slot], 2)
        right = jnp.concatenate([high, low, high], 0)
        for n, start in enumerate(range(0, 1024, CHUNK)):
            block = pl.ds(start, CHUNK)
            product = dot(lefts[slot][block], right, (1, 0))
            stage[slot, block] = (merged[slot][block] - product).astype(BF16)
            copy = pltpu.make_async_copy(stage.at[slot, block], error_hbm.at[0, m, block], sems.at[slot, n])
            copy.start()
            copies.append(copy)
        outs.append(dot(rows[slot][...].astype(BF16), right, (1, 0)))
    return copies, outs


def finish_own_kernel(scalars_ref, *refs):
    merged, lefts, rows, q_ref, error_hbm, out_ref, stage, sems = refs[:2], refs[2:4], refs[4:6], *refs[6:]
    copies, outs = finish_kernel(1, scalars_ref, merged, lefts, q_ref, rows, error_hbm, stage, sems)
    for slot in range(2):
        out_ref[slot] = outs[slot]
    for copy in copies:
        copy.wait()


def finish_own(scalars, merged, lefts, rows, q):
    return pl.pallas_call(
        finish_own_kernel,
        out_shape=[shape(1, 4, 1024, 1024, dtype=BF16), shape(2, 8, 1024)],
        in_specs=[SMEM] + [VMEM] * 7,
        out_specs=[HBM, VMEM],
        scratch_shapes=[pltpu.VMEM((2, 1024, 1024), BF16), pltpu.SemaphoreType.DMA((2, 1024 // CHUNK))],
        compiler_params=params(8),
        cost_estimate=cost(2 * 2 * 256 * 1024 * 1024, 4),
    )(scalars, *merged, *lefts, *rows, q)


def finish_other_kernel(scalars_ref, earlier_ref, *refs):
    merged, lefts, rows, q_ref, own_q_ref, own_rows = refs[:2], refs[2:4], refs[4:6], *refs[6:9]
    error_hbm, update_hbm, new_q_hbm, update, stage, sems, q_sems, update_sem = refs[9:]
    copies = []
    for side, source in enumerate((q_ref, own_q_ref)):
        place = pl.ds(members(scalars_ref, side)[0], 2)
        copies.append(pltpu.make_async_copy(source, new_q_hbm.at[place], q_sems.at[side]))
    for copy in copies:
        copy.start()
    more, outs = finish_kernel(0, scalars_ref, merged, lefts, q_ref, rows, error_hbm, stage, sems)
    for side, values in enumerate((outs, (own_rows[0], own_rows[1]))):
        for m, value in zip(members(scalars_ref, side), values):
            update[m] = value.astype(BF16)
    copies += [*more, pltpu.make_async_copy(update, update_hbm, update_sem)]
    copies[-1].start()
    for copy in copies:
        copy.wait()


def finish_other(scalars, error, merged, lefts, rows, q, own_q, own_rows):
    return pl.pallas_call(
        finish_other_kernel,
        out_shape=[shape(1, 4, 1024, 1024, dtype=BF16), shape(4, 8, 1024, dtype=BF16), shape(4, 32, 1024)],
        in_specs=[SMEM, HBM] + [VMEM] * 9,
        out_specs=[HBM, HBM, HBM],
        scratch_shapes=[
            pltpu.VMEM((4, 8, 1024), BF16),
            pltpu.VMEM((2, 1024, 1024), BF16),
            pltpu.SemaphoreType.DMA((2, 1024 // CHUNK)),
            pltpu.SemaphoreType.DMA((2,)),
            pltpu.SemaphoreType.DMA,
        ],
        input_output_aliases={1: 0},
        compiler_params=params(8),
        cost_estimate=cost(2 * 2 * 256 * 1024 * 1024, 4),
    )(scalars, error, *merged, *lefts, *rows, q, own_q, own_rows)


def add_kernel(count, scale, *refs):
    values = [ref[...] for ref in refs[:count]]
    while len(values) > 1:
        values = [values[n] + values[n + 1] for n in range(0, len(values), 2)]
    refs[-1][...] = values[0] * scale


def add(values, after=(), scale=1.0):
    return pl.pallas_call(
        lambda *refs: add_kernel(len(values), scale, *refs),
        out_shape=shape(2, 32, 1024),
        in_specs=[VMEM] * len(values) + [ANY] * len(after),
        out_specs=VMEM,
        compiler_params=params(4),
        cost_estimate=cost(65536, 0.375),
    )(*values, *after)


def received(step, value):
    return [lax.ppermute(value, AXES, step_pairs(step, mask)) for mask in (1, 3, 2)]


def on_device(inputs, cotangents, error_buffer, previous_q):
    scalars = jnp.stack([lax.axis_index("row") % 2, lax.axis_index(AXES)]).astype(jnp.int32)
    arrays = [pltpu.with_memory_space_constraint(a, pltpu.HBM) for a in (inputs, cotangents, error_buffer, previous_q)]
    *other_held, other = load(0, scalars, arrays)
    *own_held, own = load(1, scalars, arrays)
    total = add([own, other_core(other)])
    merged = {}
    for step in range(3):
        came = received(step, total)
        fill = []
        if step < 2:
            fill = [merge(slot, other_held if step else own_held, total) for slot in range(2)]
            merged[1 - step] = fill
        total = add([total, *came], fill, 1.0 / 128.0 if step == 2 else 1.0)
    mean = total
    other_mean = other_core(mean)
    own = project(own_held, mean, mean)
    other = project(other_held, other_mean, own)
    total = add([own, other_core(other)])
    for step in range(3):
        came = received(step, total)
        fill = []
        if step == 0:
            solved = [gram_schmidt(slot, mean, total) for slot in range(2)]
            basis, factors = zip(*solved)
            other_basis = [other_core(b) for b in basis]
            fill = list(basis)
        elif step == 1:
            own_flip, other_flip = flip(scalars, basis, total), flip(scalars, other_basis, total)
            fill = [own_flip[0], other_flip[0]]
        total = add([total, *came], fill)
    own_q = solve(total, factors)
    other_q = other_core(own_q)
    error, own_rows = finish_own(scalars, merged[1], own_flip[:2], own_flip[2:], own_q)
    return finish_other(scalars, error, merged[0], other_flip[:2], other_flip[2:], other_q, own_q, own_rows)


def solution(mesh):
    return jax.shard_map(
        on_device,
        mesh=mesh,
        in_specs=(
            P(None, AXES, None),
            P(None, AXES, None),
            P(AXES, None, None, None),
            P(),
        ),
        out_specs=(P(AXES, None, None, None), P(None, AXES, None), P()),
        check_vma=False,
    )
```

```python
import jax
import jax.numpy as jnp
from jax import lax
from jax.experimental import pallas as pl
from jax.experimental.pallas import tpu as pltpu
from jax.sharding import PartitionSpec as P

AXES = ("row", "col")
SIZES = (("zh", 2), ("y", 4), ("core", 2), ("x", 4), ("zl", 2))
ORDERS = (("x", "y", "z"), ("y", "z", "x"))


def coords_of(index):
    coords = {}
    for name, size in reversed(SIZES):
        coords[name] = index % size
        index //= size
    return coords


def index_of(coords):
    index = 0
    for name, size in SIZES:
        index = index * size + coords[name]
    return index


def partner(index, axis, mask):
    coords = coords_of(index)
    if axis == "z":
        z = (2 * coords["zh"] + coords["zl"]) ^ mask
        coords["zh"], coords["zl"] = z // 2, z % 2
    else:
        coords[axis] ^= mask
    return index_of(coords)


def step_pairs(step, mask):
    return [(index, partner(index, ORDERS[coords_of(index)["core"]][step], mask)) for index in range(128)]


def core_pairs():
    pairs = []
    for index in range(128):
        coords = coords_of(index)
        coords["core"] ^= 1
        pairs.append((index, index_of(coords)))
    return pairs


def other_core(value):
    return lax.ppermute(value, AXES, core_pairs())


MIB = 1024 * 1024
VMEM = pl.BlockSpec(memory_space=pltpu.VMEM)
HBM = pl.BlockSpec(memory_space=pltpu.HBM)
ANY = pl.BlockSpec(memory_space=pl.ANY)
SMEM = pl.BlockSpec(memory_space=pltpu.SMEM)
CHUNK = 256
BLOCK = 256
F32 = jnp.float32
BF16 = jnp.bfloat16


def shape(*dims, dtype=F32):
    return jax.ShapeDtypeStruct(dims, dtype)


def params(mib):
    return pltpu.CompilerParams(vmem_limit_bytes=mib * MIB)


def cost(flops, mib):
    return pl.CostEstimate(flops=flops, bytes_accessed=int(mib * MIB), transcendentals=0)


def terms(value, count):
    parts = []
    for _ in range(count):
        part = value.astype(BF16)
        parts.append(part)
        value = value - part.astype(F32)
    return parts


def split(value, count):
    return jnp.concatenate(terms(value, count), 0)


def folded(value, count):
    rows = value.shape[0] // count
    total = value[:rows]
    for n in range(1, count):
        total = total + value[n * rows : (n + 1) * rows]
    return total


def dot(a, b, contract):
    return lax.dot_general(a, b, ((contract[:1], contract[1:]), ((), ())), preferred_element_type=F32)


def members(scalars_ref, side):
    core = scalars_ref[0]
    first = 2 * core if side else 2 * (1 - core)
    return first, first + 1


def load_kernel(side, scalars_ref, x_hbm, c_hbm, e_hbm, q_hbm, x_ref, c_ref, e_ref, p_ref, q_ref, sems):
    copies = []
    for slot, m in enumerate(members(scalars_ref, side)):
        parts = [
            (q_hbm.at[m], q_ref.at[slot]),
            (c_hbm.at[m], c_ref.at[slot]),
            (x_hbm.at[m], x_ref.at[slot]),
        ] + [(e_hbm.at[0, m, pl.ds(n, 512)], e_ref.at[slot, pl.ds(n, 512)]) for n in range(0, 1024, 512)]
        started = []
        for n, (source, target) in enumerate(parts):
            copy = pltpu.make_async_copy(source, target, sems.at[slot, n])
            copy.start()
            started.append(copy)
        copies.append(started)
    for slot in range(2):
        copies[slot][0].wait()
        q = split(q_ref[slot], 3)
        copies[slot][1].wait()
        y = split(folded(dot(q, c_ref[slot], (1, 1)), 3), 3)
        copies[slot][2].wait()
        p_ref[slot] = folded(dot(y, x_ref[slot], (1, 0)), 3)
        for n in range(2):
            copies[slot][3 + n].wait()
            rows = pl.ds(512 * n, 512)
            p_ref[slot, :, rows] += folded(dot(q, e_ref[slot, rows], (1, 1)), 3)


def load(side, scalars, arrays):
    return pl.pallas_call(
        lambda *refs: load_kernel(side, *refs),
        out_shape=[
            pltpu.VMEM((2, 512, 1024), BF16),
            pltpu.VMEM((2, 512, 1024), BF16),
            pltpu.VMEM((2, 1024, 1024), BF16),
            shape(2, 32, 1024),
        ],
        in_specs=[SMEM, HBM, HBM, HBM, HBM],
        out_specs=[VMEM] * 4,
        scratch_shapes=[pltpu.VMEM((2, 32, 1024), F32), pltpu.SemaphoreType.DMA((2, 5))],
        compiler_params=params(6),
        cost_estimate=cost(2 * 2 * 96 * 1024 * 2048, 9),
    )(scalars, *arrays)


def project_kernel(slots, first_ref, second_ref, c_ref, e_ref, p_ref, after_ref, z_ref):
    turned = (first_ref, second_ref)
    for n, slot in enumerate(slots):
        p = split(p_ref[slot], 3)
        w = split(folded(dot(p, turned[slot][...], (1, 0)), 3), 3)
        z_ref[n] = folded(dot(w, c_ref[slot], (1, 0)) + dot(p, e_ref[slot], (1, 0)), 3)


def project(turned, held, p, after, slots=(0, 1)):
    return pl.pallas_call(
        lambda *refs: project_kernel(slots, *refs),
        out_shape=shape(len(slots), 32, 1024),
        in_specs=[VMEM] * 5 + [ANY],
        out_specs=VMEM,
        compiler_params=params(6),
        cost_estimate=cost(len(slots) * 2 * 96 * 1024 * 2048, 4 * len(slots)),
    )(*turned, *held[1:], p, after)


def gram_schmidt_kernel(slot, p_ref, after_ref, basis_ref, factor_ref):
    value = p_ref[slot]
    rows = lax.broadcasted_iota(jnp.int32, (32, 128), 0)
    lanes = lax.broadcasted_iota(jnp.int32, (32, 128), 1)
    factor = jnp.where(rows == lanes, 1.0, 0.0)
    for k in range(32):
        group = k // 8 * 8
        if k % 8 == 0 and k > 0:
            value, factor = value[8:], factor[8:]
        at = k - group
        row, factor_row = value[at : at + 1], factor[at : at + 1]
        dots = jnp.sum(value * row, axis=1, keepdims=True)
        square = dots[at : at + 1] + 1e-6
        scale = 1.0 / jnp.sqrt(square)
        basis_ref[k : k + 1, :] = row * scale
        factor_ref[k : k + 1, :] = factor_row * scale
        weights = dots * (1.0 / square)
        value = value - weights * row
        factor = factor - weights * factor_row


def gram_schmidt(slot, p, after):
    return pl.pallas_call(
        lambda *refs: gram_schmidt_kernel(slot, *refs),
        out_shape=[shape(32, 1024), shape(32, 128)],
        in_specs=[VMEM, ANY],
        out_specs=[VMEM, VMEM],
        compiler_params=params(4),
        cost_estimate=cost(4_000_000, 8),
    )(p, after)


def flip_kernel(scalars_ref, first_ref, second_ref, after_ref, first_left, second_left, first_rows, second_rows, flipped):
    start = pl.multiple_of(scalars_ref[1] * 8, 8)
    for basis_ref, left_ref, rows_ref in ((first_ref, first_left, first_rows), (second_ref, second_left, second_rows)):
        flipped[...] = basis_ref[...].T
        high, low = terms(flipped[...], 2)
        left_ref[...] = jnp.concatenate([high, high, low], 1)
        high, low = terms(flipped[pl.ds(start, 8), :], 2)
        rows_ref[...] = jnp.concatenate([high, high, low], 1).astype(F32)


def flip(scalars, bases, after):
    return pl.pallas_call(
        flip_kernel,
        out_shape=[shape(1024, 96, dtype=BF16)] * 2 + [shape(8, 96)] * 2,
        in_specs=[SMEM, VMEM, VMEM, ANY],
        out_specs=[VMEM] * 4,
        scratch_shapes=[pltpu.VMEM((1024, 32), F32)],
        compiler_params=params(4),
        cost_estimate=cost(1_000_000, 3),
    )(scalars, *bases, after)


def merge_kernel(slot, x_ref, c_ref, e_ref, after_ref, merged_ref, turned_ref):
    for start in range(0, 1024, CHUNK):
        rows = pl.ds(start, CHUNK)
        turned_ref[rows] = x_ref[slot, :, rows].T
        merged_ref[rows] = dot(turned_ref[rows], c_ref[slot], (1, 0)) + e_ref[slot, rows].astype(F32)


def merge(slot, held, after):
    return pl.pallas_call(
        lambda *refs: merge_kernel(slot, *refs),
        out_shape=[pltpu.VMEM((1024, 1024), F32), pltpu.VMEM((1024, 512), BF16)],
        in_specs=[VMEM] * 3 + [ANY],
        out_specs=[VMEM, VMEM],
        compiler_params=params(6),
        cost_estimate=cost(2 * 512 * 1024 * 1024, 4),
    )(*held, after)


def solve_kernel(total_ref, first_ref, second_ref, q_ref):
    pairs = ((0, 0), (0, 1), (0, 2), (1, 0), (1, 1), (2, 0))
    for slot, factor_ref in enumerate((first_ref, second_ref)):
        f = terms(factor_ref[:, :32], 3)
        z = terms(total_ref[slot], 3)
        left = jnp.concatenate([f[i] for i, _ in pairs], 1)
        right = jnp.concatenate([z[j] for _, j in pairs], 0)
        q_ref[slot] = dot(left, right, (1, 0)) * (1.0 / 128.0)


def solve(total, factors):
    return pl.pallas_call(
        solve_kernel,
        out_shape=shape(2, 32, 1024),
        in_specs=[VMEM] * 3,
        out_specs=VMEM,
        compiler_params=params(4),
        cost_estimate=cost(2 * 2 * 32 * 192 * 1024, 1),
    )(total, *factors)


def finish_kernel(side, scalars_ref, merged, lefts, q_ref, rows, error_hbm, stage, sems):
    copies, outs = [], []
    for slot, m in enumerate(members(scalars_ref, side)):
        high, low = terms(q_ref[slot], 2)
        right = jnp.concatenate([high, low, high], 0)
        for n, start in enumerate(range(0, 1024, BLOCK)):
            block = pl.ds(start, BLOCK)
            product = dot(lefts[slot][block], right, (1, 0))
            stage[slot, block] = (merged[slot][block] - product).astype(BF16)
            copy = pltpu.make_async_copy(stage.at[slot, block], error_hbm.at[0, m, block], sems.at[slot, n])
            copy.start()
            copies.append(copy)
        outs.append(dot(rows[slot][...].astype(BF16), right, (1, 0)))
    return copies, outs


def finish_own_kernel(scalars_ref, *refs):
    merged, lefts, rows, q_ref, error_hbm, out_ref, stage, sems = refs[:2], refs[2:4], refs[4:6], *refs[6:]
    copies, outs = finish_kernel(1, scalars_ref, merged, lefts, q_ref, rows, error_hbm, stage, sems)
    for slot in range(2):
        out_ref[slot] = outs[slot]
    for copy in copies:
        copy.wait()


def finish_own(scalars, merged, lefts, rows, q):
    return pl.pallas_call(
        finish_own_kernel,
        out_shape=[shape(1, 4, 1024, 1024, dtype=BF16), shape(2, 8, 1024)],
        in_specs=[SMEM] + [VMEM] * 7,
        out_specs=[HBM, VMEM],
        scratch_shapes=[pltpu.VMEM((2, 1024, 1024), BF16), pltpu.SemaphoreType.DMA((2, 1024 // BLOCK))],
        compiler_params=params(8),
        cost_estimate=cost(2 * 2 * 256 * 1024 * 1024, 4),
    )(scalars, *merged, *lefts, *rows, q)


def finish_other_kernel(scalars_ref, earlier_ref, *refs):
    merged, lefts, rows, q_ref, own_q_ref, own_rows = refs[:2], refs[2:4], refs[4:6], *refs[6:9]
    error_hbm, update_hbm, new_q_hbm, update, stage, sems, q_sems, update_sem = refs[9:]
    copies = []
    for side, source in enumerate((q_ref, own_q_ref)):
        place = pl.ds(members(scalars_ref, side)[0], 2)
        copies.append(pltpu.make_async_copy(source, new_q_hbm.at[place], q_sems.at[side]))
    for copy in copies:
        copy.start()
    more, outs = finish_kernel(0, scalars_ref, merged, lefts, q_ref, rows, error_hbm, stage, sems)
    for side, values in enumerate((outs, (own_rows[0], own_rows[1]))):
        for m, value in zip(members(scalars_ref, side), values):
            update[m] = value.astype(BF16)
    copies += [*more, pltpu.make_async_copy(update, update_hbm, update_sem)]
    copies[-1].start()
    for copy in copies:
        copy.wait()


def finish_other(scalars, error, merged, lefts, rows, q, own_q, own_rows):
    return pl.pallas_call(
        finish_other_kernel,
        out_shape=[shape(1, 4, 1024, 1024, dtype=BF16), shape(4, 8, 1024, dtype=BF16), shape(4, 32, 1024)],
        in_specs=[SMEM, HBM] + [VMEM] * 9,
        out_specs=[HBM, HBM, HBM],
        scratch_shapes=[
            pltpu.VMEM((4, 8, 1024), BF16),
            pltpu.VMEM((2, 1024, 1024), BF16),
            pltpu.SemaphoreType.DMA((2, 1024 // BLOCK)),
            pltpu.SemaphoreType.DMA((2,)),
            pltpu.SemaphoreType.DMA,
        ],
        input_output_aliases={1: 0},
        compiler_params=params(8),
        cost_estimate=cost(2 * 2 * 256 * 1024 * 1024, 4),
    )(scalars, error, *merged, *lefts, *rows, q, own_q, own_rows)


def add_kernel(count, scale, *refs):
    values = [ref[...] for ref in refs[:count]]
    while len(values) > 1:
        values = [values[n] + values[n + 1] for n in range(0, len(values), 2)]
    refs[-1][...] = values[0] * scale


def add(values, after=(), scale=1.0):
    return pl.pallas_call(
        lambda *refs: add_kernel(len(values), scale, *refs),
        out_shape=shape(2, 32, 1024),
        in_specs=[VMEM] * len(values) + [ANY] * len(after),
        out_specs=VMEM,
        compiler_params=params(4),
        cost_estimate=cost(65536, 0.375),
    )(*values, *after)


def received(step, value):
    return [lax.ppermute(value, AXES, step_pairs(step, mask)) for mask in (2, 3, 1)]


def on_device(inputs, cotangents, error_buffer, previous_q):
    scalars = jnp.stack([lax.axis_index("row") % 2, lax.axis_index(AXES)]).astype(jnp.int32)
    arrays = [pltpu.with_memory_space_constraint(a, pltpu.HBM) for a in (inputs, cotangents, error_buffer, previous_q)]
    *other_held, other = load(0, scalars, arrays)
    *own_held, own = load(1, scalars, arrays)
    total = add([own, other_core(other)])
    merged, turned = {}, {}
    for step in range(3):
        came = received(step, total)
        fill = []
        if step < 2:
            merged[1 - step], turned[1 - step] = zip(*(merge(slot, other_held if step else own_held, total) for slot in range(2)))
            fill = merged[1 - step]
        total = add([total, *came], tuple(fill), 1.0 / 128.0 if step == 2 else 1.0)
    mean = total
    other_mean = other_core(mean)
    own = project(turned[1], own_held, mean, mean)
    other = project(turned[0], other_held, other_mean, own)
    total = add([own, other_core(other)])
    for step in range(3):
        came = received(step, total)
        fill = []
        if step == 0:
            solved = [gram_schmidt(slot, mean, total) for slot in range(2)]
            basis, factors = zip(*solved)
            other_basis = [other_core(b) for b in basis]
            fill = list(basis)
        elif step == 1:
            own_flip, other_flip = flip(scalars, basis, total), flip(scalars, other_basis, total)
            fill = [own_flip[0], other_flip[0]]
        total = add([total, *came], fill)
    own_q = solve(total, factors)
    other_q = other_core(own_q)
    error, own_rows = finish_own(scalars, merged[1], own_flip[:2], own_flip[2:], own_q)
    return finish_other(scalars, error, merged[0], other_flip[:2], other_flip[2:], other_q, own_q, own_rows)


def solution(mesh):
    return jax.shard_map(
        on_device,
        mesh=mesh,
        in_specs=(
            P(None, AXES, None),
            P(None, AXES, None),
            P(AXES, None, None, None),
            P(),
        ),
        out_specs=(P(AXES, None, None, None), P(None, AXES, None), P()),
        check_vma=False,
    )
```
